128 devices in a mesh: frames: 4 (over z_lo, core), feat: 32 (over z_hi, y, x).
Axes of the slice: x: 4, y: 4, z: 4 (z_hi: 2, z_lo: 2; z = z_hi * 2 + z_lo), core: 2. Of those that a mesh axis runs over, the one named last changes fastest.
Arguments:
- trajectory: bfloat16 [1024, 212992], P(('frames', 'feat'))
- tile_list: int32 [12288, 2], P(('frames', 'feat')), may hold values from 0 to 1663, as said below
Outputs:
- cov_instant: float32 [12288, 128, 128], P(('frames', 'feat'))
- cov_lagged: float32 [12288, 128, 128], P(('frames', 'feat'))
The draws below stay inside these ranges and needn't reach their ends.
Inputs may be any that keep to these rules, and one draw needn't show every extreme that they name: `tile_list`: the tiles of device d (entries d * 96 to (d + 1) * 96 - 1) have row blocks I from d * 13 - 2 to (d + 1) * 13 + 1 and column blocks J with |I - J| <= 4, all within 0 to 1663; tiles may repeat.
All inputs are finite; a program needn't handle non-finite values.
Results may differ from the reference program's by a relative error of at most 0.004.
Values may be sent and summed in bfloat16 or wider, within the bound.
No kernel may reach another device: no remote copies, remote signals or barrier semaphores. Data moves between devices by JAX's collectives and lax.ppermute only.
A program may use at most 128 MiB of HBM per device.

```python
import math
import jax
import jax.numpy as jnp
from jax import lax

BS = 128
BLK_DEV = 13
NBLK = 1664
FEATURES = 212992
FRAMES = 1024
LAG = 16
BAND = 4
REACH = 2
TILES_DEV = 96
NTILES = 12288


def draw_trajectory(key, part):
    noise_key = jax.random.fold_in(key, 11)
    scale_key = jax.random.fold_in(key, 12)
    frame_key = jax.random.fold_in(key, 13)
    centre_key = jax.random.fold_in(key, 14)
    jitter = jax.random.normal(noise_key, (FRAMES, FEATURES), jnp.float32)
    feat_scale = jnp.exp(jax.random.uniform(scale_key, (FEATURES,), jnp.float32, math.log(0.25), math.log(2.5)))
    frame_scale = jnp.exp(jax.random.uniform(frame_key, (FRAMES, 1), jnp.float32, math.log(0.5), math.log(2.0)))
    centre = jax.random.uniform(centre_key, (FEATURES,), jnp.float32, -2.0, 2.0)
    return (centre + feat_scale * frame_scale * jitter).astype(jnp.bfloat16)


def draw_tile_list(key, part):
    row_key = jax.random.fold_in(key, 21)
    offset_key = jax.random.fold_in(key, 22)
    position = jnp.arange(NTILES, dtype=jnp.int32)
    owner_device = position // TILES_DEV
    slot_index = position % TILES_DEV
    row_index = owner_device * BLK_DEV - REACH + jax.random.randint(row_key, (NTILES,), 0, BLK_DEV + 2 * REACH, jnp.int32)
    offset = jax.random.randint(offset_key, (NTILES,), -BAND, BAND + 1, jnp.int32)
    row_index = jnp.where(slot_index == 0, owner_device * BLK_DEV - REACH, row_index)
    row_index = jnp.where(slot_index == 1, (owner_device + 1) * BLK_DEV + REACH - 1, row_index)
    offset = jnp.where(slot_index == 0, -BAND, jnp.where(slot_index == 1, BAND, offset))
    row_index = jnp.clip(row_index, 0, NBLK - 1)
    col_index = jnp.clip(row_index + offset, 0, NBLK - 1)
    return jnp.stack([row_index, col_index], axis=1).astype(jnp.int32)


def setup_inputs(seed: int = 0) -> dict:
    splits = jax.random.split(jax.random.key(seed), 3)
    trajectory = draw_trajectory(jax.random.fold_in(splits[2], 71), 0)
    tile_list = draw_tile_list(jax.random.fold_in(splits[2], 71), 0)
    return dict(trajectory=trajectory, tile_list=tile_list)


def reference(trajectory, tile_list):
    column_means = jnp.sum(trajectory.astype(jnp.float32), axis=0) / FRAMES
    centred = (trajectory.astype(jnp.float32) - column_means).astype(jnp.bfloat16)
    panels = centred.reshape(FRAMES, NBLK, BS)
    groups = tile_list.reshape(-1, 64, 2)

    def tile_group(members):
        row_panels = jnp.take(panels, members[:, 0], axis=1).astype(jnp.float32)
        col_panels = jnp.take(panels, members[:, 1], axis=1).astype(jnp.float32)
        instant = jnp.einsum("tgi,tgj->gij", row_panels, col_panels, precision=lax.Precision.HIGHEST)
        lagged = jnp.einsum("tgi,tgj->gij", row_panels[:FRAMES - LAG], col_panels[LAG:], precision=lax.Precision.HIGHEST)
        return instant / (FRAMES - 1), lagged / (FRAMES - LAG)

    instant, lagged = lax.map(tile_group, groups)
    return instant.reshape(NTILES, BS, BS), lagged.reshape(NTILES, BS, BS)
```

```python
import functools

import jax
import jax.numpy as jnp
from jax import lax
from jax.experimental import pallas as pl
from jax.experimental.pallas import tpu as pltpu
from jax.sharding import PartitionSpec as P

BS = 128
LAG = 16
BAND = 4
REACH = 2
MARGIN = REACH + BAND
SPAN = 2 * BAND + 1
EDGE = MARGIN + BAND
ROWS = REACH + BAND
AXES = ("frames", "feat")
F32 = jnp.float32
BF16 = jnp.bfloat16


def pair_into(pair_ref, slot, panel):
    frames = panel.shape[0]
    pair_ref[slot, :, :BS] = panel
    pair_ref[slot, : frames - LAG, BS:] = panel[LAG:]
    pair_ref[slot, frames - LAG :, BS:] = jnp.zeros((LAG, BS), BF16)


def send_tiles(place_ref, res_i, res_l, out_i, out_l, sems):
    tiles = place_ref.shape[0]

    def copies(k):
        at = place_ref[k]
        return (
            pltpu.make_async_copy(res_i.at[at], out_i.at[k], sems.at[k, 0]),
            pltpu.make_async_copy(res_l.at[at], out_l.at[k], sems.at[k, 1]),
        )

    @pl.loop(0, tiles)
    def _(k):
        @pl.when(place_ref[k] >= 0)
        def _():
            for copy in copies(k):
                copy.start()

    @pl.loop(0, tiles)
    def _(k):
        @pl.when(place_ref[k] >= 0)
        def _():
            for copy in copies(k):
                copy.wait()


def inner_kernel(blocks, place_ref, left_ref, mid_ref, right_ref, out_i, out_l, turned, pair, res_i, res_l, sems):
    frames = left_ref.shape[0]
    wide = left_ref.shape[1] // BS
    for b in range(blocks):
        if b < wide:
            panel = left_ref[:, b * BS : (b + 1) * BS]
        elif b < blocks - wide:
            panel = mid_ref[:, (b - wide) * BS : (b - wide + 1) * BS]
        else:
            c = b - (blocks - wide)
            panel = right_ref[:, c * BS : (c + 1) * BS]
        turned[b * BS : (b + 1) * BS, :] = panel.T
        pair_into(pair, b, panel)

    @pl.loop(0, blocks)
    def _(j):
        first = jnp.clip(j - BAND, 0, blocks - SPAN)
        for i in range(SPAN):
            rows = turned[pl.ds(pl.multiple_of((first + i) * BS, BS), BS), :]
            prod = jnp.dot(rows, pair[j], preferred_element_type=F32)
            res_i[j * SPAN + i] = prod[:, :BS] * (1.0 / (frames - 1))
            res_l[j * SPAN + i] = prod[:, BS:] * (1.0 / (frames - LAG))

    send_tiles(place_ref, res_i, res_l, out_i, out_l, sems)


def edge_kernel(
    place_ref, from_left, left_ref, right_ref, from_right, in_i, in_l, out_i, out_l, turned, pair, res_i, res_l, sems
):
    del in_i, in_l
    frames = left_ref.shape[0]

    def block(ref, b):
        return ref[:, b * BS : (b + 1) * BS]

    wide = left_ref.shape[1] // BS
    for side in range(2):
        if side == 0:
            cols = [block(from_left, b) for b in range(MARGIN)] + [block(left_ref, b) for b in range(BAND)]
            row0 = MARGIN - REACH
        else:
            cols = [block(right_ref, wide - BAND + b) for b in range(BAND)] + [block(from_right, b) for b in range(MARGIN)]
            row0 = 0
        for r in range(ROWS):
            turned[r * BS : (r + 1) * BS, :] = cols[row0 + r].T
        for c in range(EDGE):
            pair_into(pair, c, cols[c])
        for c in range(EDGE):
            if side == 0:
                own_col = c >= MARGIN
                keep = [r for r in range(ROWS) if abs(r + row0 - c) <= BAND and (r < REACH or not own_col)]
            else:
                own_col = c < BAND
                keep = [r for r in range(ROWS) if abs(r + row0 - c) <= BAND and (r >= BAND or not own_col)]
            lo, hi = keep[0], keep[-1] + 1
            prod = jnp.dot(turned[lo * BS : hi * BS, :], pair[c], preferred_element_type=F32)
            for r in range(lo, hi):
                part = prod[(r - lo) * BS : (r - lo + 1) * BS]
                at = side * ROWS * EDGE + r * EDGE + c
                res_i[at] = part[:, :BS] * (1.0 / (frames - 1))
                res_l[at] = part[:, BS:] * (1.0 / (frames - LAG))

    send_tiles(place_ref, res_i, res_l, out_i, out_l, sems)


def per_device(trajectory, tile_list):
    panels = lax.all_to_all(trajectory, AXES, split_axis=1, concat_axis=0, tiled=True)
    frames = panels.shape[0]
    blocks = panels.shape[1] // BS
    tiles = tile_list.shape[0]
    count = lax.axis_size(AXES)

    rel = tile_list - lax.axis_index(AXES) * blocks
    row, col = rel[:, 0], rel[:, 1]
    on_left = (row < 0) | (col < 0)
    on_right = (row >= blocks) | (col >= blocks)
    inner_place = jnp.where(on_left | on_right, -1, col * SPAN + row - jnp.clip(col - BAND, 0, blocks - SPAN))
    left_place = (row + REACH) * EDGE + col + MARGIN
    right_place = ROWS * EDGE + (row - (blocks - BAND)) * EDGE + col - (blocks - BAND)
    edge_place = jnp.where(on_left, left_place, jnp.where(on_right, right_place, -1))

    column_means = jnp.sum(panels, axis=0, dtype=F32) / frames

    def centred(lo, hi):
        return (panels[:, lo * BS : hi * BS] - column_means[lo * BS : hi * BS]).astype(BF16)

    left = centred(0, MARGIN)
    right = centred(blocks - MARGIN, blocks)
    mid = centred(MARGIN, blocks - MARGIN)
    from_right = lax.ppermute(left, AXES, [(i + 1, i) for i in range(count - 1)])
    from_left = lax.ppermute(right, AXES, [(i, i + 1) for i in range(count - 1)])

    vmem = pl.BlockSpec(memory_space=pltpu.VMEM)
    smem = pl.BlockSpec(memory_space=pltpu.SMEM)
    hbm = pl.BlockSpec(memory_space=pl.ANY)
    outs = [jax.ShapeDtypeStruct((tiles, BS, BS), F32)] * 2
    inner = pl.pallas_call(
        functools.partial(inner_kernel, blocks),
        out_shape=outs,
        in_specs=[smem, vmem, vmem, vmem],
        out_specs=[hbm, hbm],
        scratch_shapes=[
            pltpu.VMEM((blocks * BS, frames), BF16),
            pltpu.VMEM((blocks, frames, 2 * BS), BF16),
            pltpu.VMEM((blocks * SPAN, BS, BS), F32),
            pltpu.VMEM((blocks * SPAN, BS, BS), F32),
            pltpu.SemaphoreType.DMA((tiles, 2)),
        ],
        compiler_params=pltpu.CompilerParams(vmem_limit_bytes=44 << 20),
        cost_estimate=pl.CostEstimate(
            flops=2 * blocks * SPAN * BS * BS * frames * 2, bytes_accessed=16 << 20, transcendentals=0
        ),
        name="inner_tiles",
    )
    inst, lagg = inner(inner_place, left, mid, right)
    edge = pl.pallas_call(
        edge_kernel,
        out_shape=outs,
        in_specs=[smem, vmem, vmem, vmem, vmem, hbm, hbm],
        out_specs=[hbm, hbm],
        scratch_shapes=[
            pltpu.VMEM((ROWS * BS, frames), BF16),
            pltpu.VMEM((EDGE, frames, 2 * BS), BF16),
            pltpu.VMEM((2 * ROWS * EDGE, BS, BS), F32),
            pltpu.VMEM((2 * ROWS * EDGE, BS, BS), F32),
            pltpu.SemaphoreType.DMA((tiles, 2)),
        ],
        input_output_aliases={5: 0, 6: 1},
        compiler_params=pltpu.CompilerParams(vmem_limit_bytes=44 << 20),
        cost_estimate=pl.CostEstimate(
            flops=2 * 56 * BS * BS * frames * 2, bytes_accessed=16 << 20, transcendentals=0
        ),
        name="edge_tiles",
    )
    inst, lagg = edge(edge_place, from_left, left, right, from_right, inst, lagg)
    return (inst, lagg)


def solution(mesh):
    in_specs = (P(AXES, None), P(AXES, None))
    out_specs = (P(AXES, None, None), P(AXES, None, None))
    return jax.shard_map(per_device, mesh=mesh, in_specs=in_specs, out_specs=out_specs, check_vma=False)
```

```python
import functools

import jax
import jax.numpy as jnp
from jax import lax
from jax.experimental import pallas as pl
from jax.experimental.pallas import tpu as pltpu
from jax.sharding import PartitionSpec as P

BS = 128
LAG = 16
BAND = 4
REACH = 2
HALO = 4
SPAN = 2 * BAND + 1
ROWS = REACH + BAND
COLS = HALO + BAND
SLOT = 128
AXES = ("frames", "feat")
F32 = jnp.float32
BF16 = jnp.bfloat16
VMEM = pl.BlockSpec(memory_space=pltpu.VMEM)
SMEM = pl.BlockSpec(memory_space=pltpu.SMEM)
HBM = pl.BlockSpec(memory_space=pl.ANY)


def far_tiles(blocks):
    low, high = [], []
    for col in range(HALO, REACH + BAND):
        low.append((col, list(range(max(0, col - BAND), REACH))))
    for col in range(blocks - 1 - HALO, blocks - 1 - REACH - BAND, -1):
        high.append((col, list(range(blocks - REACH, min(blocks, col + BAND + 1)))))
    return low, high


def far_count():
    reach = REACH + BAND - HALO
    return reach * (reach + 1) // 2


def centred(panels_ref, b):
    panel = panels_ref[:, b * BS : (b + 1) * BS].astype(F32)
    mean = jnp.sum(panel, axis=0, keepdims=True) * (1.0 / panel.shape[0])
    return (panel - mean).astype(BF16)


def pair_into(pair_ref, slot, panel):
    frames = panel.shape[0]
    pair_ref[slot, :, :BS] = panel
    pair_ref[slot, : frames - LAG, BS:] = panel[LAG:]
    pair_ref[slot, frames - LAG :, BS:] = jnp.zeros((LAG, BS), BF16)


def block_rows(first, last):
    return slice(first * BS, last * BS)


def copies(key, res, out_i, out_l, sems, base):
    at = lax.shift_right_logical(key, 7) - base
    tile = lax.bitwise_and(key, SLOT - 1)
    return (
        pltpu.make_async_copy(res.at[at, 0], out_i.at[tile], sems.at[tile, 0]),
        pltpu.make_async_copy(res.at[at, 1], out_l.at[tile], sems.at[tile, 1]),
    )


def start_run(keys_ref, first, last, *where):
    @pl.loop(first, last)
    def _(r):
        for copy in copies(keys_ref[r], *where):
            copy.start()


def wait_run(keys_ref, first, last, *where):
    @pl.loop(first, last)
    def _(r):
        for copy in copies(keys_ref[r], *where):
            copy.wait()


def keep(res, at, part, frames):
    res[at, 0] = part[:, :BS] * (1.0 / (frames - 1))
    res[at, 1] = part[:, BS:] * (1.0 / (frames - LAG))


def far_kernel(blocks, own_ref, low_ref, high_ref, turned, pair):
    frames = own_ref.shape[0]
    scale = jnp.where(lax.broadcasted_iota(jnp.int32, (1, 2 * BS), 1) < BS, 1.0 / (frames - 1), 1.0 / (frames - LAG))
    for side, out_ref in zip(far_tiles(blocks), (low_ref, high_ref)):
        first = min(rows[0] for _, rows in side)
        for row in sorted({row for _, rows in side for row in rows}):
            turned[block_rows(row - first, row - first + 1), :] = centred(own_ref, row).T
        at = 0
        for slot, (col, rows) in enumerate(side):
            pair_into(pair, slot, centred(own_ref, col))
            lhs = turned[block_rows(rows[0] - first, rows[-1] + 1 - first), :]
            prod = jnp.dot(lhs, pair[slot], preferred_element_type=F32)
            out_ref[block_rows(at, at + len(rows)), :] = (prod * scale).astype(BF16)
            at += len(rows)


def inner_kernel(
    blocks, groups, keys_ref, ends_ref, own_ref, out_i, out_l, rows_l, rows_r, cols_l, cols_r, turned, pair, res, sems, side_sems
):
    frames = own_ref.shape[0]
    where = (res, out_i, out_l, sems, 0)
    far = blocks - BAND
    side_copies = [
        pltpu.make_async_copy(turned.at[pl.ds(0, BAND * BS)], rows_l, side_sems.at[0]),
        pltpu.make_async_copy(turned.at[pl.ds(far * BS, BAND * BS)], rows_r, side_sems.at[1]),
        pltpu.make_async_copy(pair.at[pl.ds(0, BAND)], cols_l, side_sems.at[2]),
        pltpu.make_async_copy(pair.at[pl.ds(far, BAND)], cols_r, side_sems.at[3]),
    ]
    ready = 0
    first = 0
    for end in groups:
        for b in range(ready, min(blocks, end + BAND)):
            panel = centred(own_ref, b)
            turned[block_rows(b, b + 1), :] = panel.T
            pair_into(pair, b, panel)
        if ready < blocks <= end + BAND:
            for copy in side_copies:
                copy.start()
        ready = min(blocks, end + BAND)
        for col in range(first, end):
            low, high = max(0, col - BAND), min(blocks, col + BAND + 1)
            prod = jnp.dot(turned[block_rows(low, high), :], pair[col], preferred_element_type=F32)
            for row in range(low, high):
                keep(res, col * SPAN + row - col + BAND, prod[block_rows(row - low, row - low + 1)], frames)
        start_run(keys_ref, ends_ref[first], ends_ref[end], *where)
        first = end
    for copy in side_copies:
        copy.wait()
    wait_run(keys_ref, 0, ends_ref[blocks], *where)


def edge_kernel(
    blocks, base, keys_ref, ends_ref, far_l, far_r, rows_l, rows_r, cols_l, cols_r, halo_ref, in_i, in_l,
    out_i, out_l, raw, far, turned, pair, res, sems, in_sems,
):
    del in_i, in_l
    frames = halo_ref.shape[0]
    where = (res, out_i, out_l, sems, base)
    count = far_count()
    halo0, own0, row0 = (0, BAND), (HALO, 0), (HALO - REACH, 0)

    def halo_copy(side, b):
        at = side * HALO + b
        return pltpu.make_async_copy(halo_ref.at[:, pl.ds(at * BS, BS)], raw.at[at], in_sems.at[at])

    def side_copy(side, kind):
        src, dst = (
            ((far_l, far_r)[side], far.at[side]),
            ((rows_l, rows_r)[side], turned.at[side, pl.ds((own0[side] - row0[side]) * BS, BAND * BS)]),
            ((cols_l, cols_r)[side], pair.at[side, pl.ds(own0[side], BAND)]),
        )[kind]
        return pltpu.make_async_copy(src, dst, in_sems.at[2 * HALO + 3 * side + kind])

    for side in range(2):
        for b in range(HALO):
            halo_copy(side, b).start()
        for kind in (1, 2, 0):
            side_copy(side, kind).start()
    for side in range(2):
        for b in range(HALO):
            halo_copy(side, b).wait()
            panel = centred(raw.at[side * HALO + b], 0)
            pair_into(pair.at[side], halo0[side] + b, panel)
            row = halo0[side] + b - row0[side]
            if 0 <= row < ROWS:
                turned[side, block_rows(row, row + 1), :] = panel.T
        side_copy(side, 1).wait()
        side_copy(side, 2).wait()
        for col in range(COLS):
            rows = [row for row in range(ROWS) if abs(row + row0[side] - col) <= BAND]
            if own0[side] <= col < own0[side] + BAND:
                rows = [row for row in rows if (row < REACH if side == 0 else row >= BAND)]
            low, high = rows[0], rows[-1] + 1
            prod = jnp.dot(turned[side, block_rows(low, high), :], pair[side, col], preferred_element_type=F32)
            for row in rows:
                at = 2 * count + (side * ROWS + row) * COLS + col
                keep(res, at, prod[block_rows(row - low, row - low + 1)], frames)
        start_run(keys_ref, ends_ref[blocks + 1 + side], ends_ref[blocks + 2 + side], *where)
        if side == 0:
            for other in range(2):
                side_copy(other, 0).wait()
                for t in range(count):
                    for half in range(2):
                        part = far[other, block_rows(t, t + 1), half * BS : (half + 1) * BS]
                        res[other * count + t, half] = part.astype(F32)
            start_run(keys_ref, ends_ref[blocks], ends_ref[blocks + 1], *where)
    wait_run(keys_ref, ends_ref[blocks], keys_ref.shape[0], *where)


def sorted_keys(tile_list, blocks):
    tiles = tile_list.shape[0]
    rel = tile_list - lax.axis_index(AXES) * blocks
    row, col = rel[:, 0], rel[:, 1]
    inner = col * SPAN + row - col + BAND
    far0 = blocks * SPAN
    reach = REACH + BAND - HALO
    below = -HALO - 1 - col
    above = col - (blocks + HALO)

    def before(step):
        return step * reach - step * (step - 1) // 2

    far_low = far0 + before(below) + row + REACH
    far_high = far0 + far_count() + before(above) + row - (blocks + HALO - BAND) - above
    left0 = far0 + 2 * far_count()
    right0 = left0 + ROWS * COLS
    left = left0 + (row + REACH) * COLS + col + HALO
    right = right0 + (row - (blocks - BAND)) * COLS + col - (blocks - BAND)
    place = jnp.where((row >= blocks) | (col >= blocks), right, inner)
    place = jnp.where((row < 0) | (col < 0), left, place)
    place = jnp.where(below >= 0, far_low, jnp.where(above >= 0, far_high, place))
    key = place * SLOT + lax.iota(jnp.int32, tiles)
    rank = jnp.sum((key[None, :] < key[:, None]).astype(jnp.int32), axis=1)
    keys = jnp.sum(jnp.where(rank[None, :] == lax.iota(jnp.int32, tiles)[:, None], key[None, :], 0), axis=1)
    number = lax.iota(jnp.int32, blocks + 4)
    edges = number * SPAN
    for at, value in ((1, left0), (2, right0), (3, right0 + ROWS * COLS)):
        edges = jnp.where(number == blocks + at, value, edges)
    ends = jnp.sum((key[None, :] < edges[:, None] * SLOT).astype(jnp.int32), axis=1)
    return keys, ends, far0


def per_device(trajectory, tile_list):
    count = lax.axis_size(AXES)
    parts = trajectory.reshape(trajectory.shape[0], count, -1)
    blocks = parts.shape[2] // BS
    tiles = tile_list.shape[0]
    own = lax.all_to_all(trajectory, AXES, split_axis=1, concat_axis=0, tiled=True)
    frames = own.shape[0]
    edge = HALO * BS
    beside = jnp.concatenate(
        [
            jnp.pad(parts[:, :-1, parts.shape[2] - edge :], ((0, 0), (1, 0), (0, 0))),
            jnp.pad(parts[:, 1:, :edge], ((0, 0), (0, 1), (0, 0))),
        ],
        axis=2,
    )
    keys, ends, base = sorted_keys(tile_list, blocks)
    own, beside, keys, ends = lax.optimization_barrier((own, beside, keys, ends))
    halo = lax.all_to_all(beside, AXES, split_axis=1, concat_axis=0, tiled=True).reshape(frames, 2 * edge)

    low, high = far_tiles(blocks)
    far = far_count()
    to_left, to_right = pl.pallas_call(
        functools.partial(far_kernel, blocks),
        out_shape=[jax.ShapeDtypeStruct((far * BS, 2 * BS), BF16)] * 2,
        in_specs=[VMEM],
        out_specs=[VMEM, VMEM],
        scratch_shapes=[
            pltpu.VMEM((REACH * BS, frames), BF16),
            pltpu.VMEM((len(low), frames, 2 * BS), BF16),
        ],
        compiler_params=pltpu.CompilerParams(vmem_limit_bytes=16 << 20),
        cost_estimate=pl.CostEstimate(flops=2 * far * 4 * BS * BS * frames, bytes_accessed=6 << 20, transcendentals=0),
        name="far_tiles",
    )(own)
    far_r = lax.ppermute(to_left, AXES, [(i + 1, i) for i in range(count - 1)])
    far_l = lax.ppermute(to_right, AXES, [(i, i + 1) for i in range(count - 1)])

    outs = [jax.ShapeDtypeStruct((tiles, BS, BS), F32)] * 2
    inst, lagg, rows_l, rows_r, cols_l, cols_r = pl.pallas_call(
        functools.partial(inner_kernel, blocks, (blocks,)),
        out_shape=outs
        + [jax.ShapeDtypeStruct((BAND * BS, frames), BF16)] * 2
        + [jax.ShapeDtypeStruct((BAND, frames, 2 * BS), BF16)] * 2,
        in_specs=[SMEM, SMEM, VMEM],
        out_specs=[HBM] * 6,
        scratch_shapes=[
            pltpu.VMEM((blocks * BS, frames), BF16),
            pltpu.VMEM((blocks, frames, 2 * BS), BF16),
            pltpu.VMEM((blocks * SPAN, 2, BS, BS), F32),
            pltpu.SemaphoreType.DMA((tiles, 2)),
            pltpu.SemaphoreType.DMA((4,)),
        ],
        compiler_params=pltpu.CompilerParams(vmem_limit_bytes=58 << 20),
        cost_estimate=pl.CostEstimate(
            flops=blocks * SPAN * 4 * BS * BS * frames, bytes_accessed=20 << 20, transcendentals=0
        ),
        name="inner_tiles",
    )(keys, ends, own)
    inst, lagg = pl.pallas_call(
        functools.partial(edge_kernel, blocks, base),
        out_shape=outs,
        in_specs=[SMEM, SMEM] + [HBM] * 9,
        out_specs=[HBM, HBM],
        scratch_shapes=[
            pltpu.VMEM((2 * HALO, frames, BS), BF16),
            pltpu.VMEM((2, far * BS, 2 * BS), BF16),
            pltpu.VMEM((2, ROWS * BS, frames), BF16),
            pltpu.VMEM((2, COLS, frames, 2 * BS), BF16),
            pltpu.VMEM((2 * far + 2 * ROWS * COLS, 2, BS, BS), F32),
            pltpu.SemaphoreType.DMA((tiles, 2)),
            pltpu.SemaphoreType.DMA((2 * HALO + 6,)),
        ],
        input_output_aliases={9: 0, 10: 1},
        compiler_params=pltpu.CompilerParams(vmem_limit_bytes=58 << 20),
        cost_estimate=pl.CostEstimate(flops=50 * 4 * BS * BS * frames, bytes_accessed=16 << 20, transcendentals=0),
        name="edge_tiles",
    )(keys, ends, far_l, far_r, rows_l, rows_r, cols_l, cols_r, halo, inst, lagg)
    return (inst, lagg)


def solution(mesh):
    in_specs = (P(AXES, None), P(AXES, None))
    out_specs = (P(AXES, None, None), P(AXES, None, None))
    return jax.shard_map(per_device, mesh=mesh, in_specs=in_specs, out_specs=out_specs, check_vma=False)
```

```python
import functools

import jax
import jax.numpy as jnp
from jax import lax
from jax.experimental import pallas as pl
from jax.experimental.pallas import tpu as pltpu
from jax.sharding import PartitionSpec as P

BS = 128
LAG = 16
BAND = 4
REACH = 2
HALO = 4
SPAN = 2 * BAND + 1
ROWS = REACH + BAND
COLS = HALO + BAND
SLOT = 128
AXES = ("frames", "feat")
F32 = jnp.float32
BF16 = jnp.bfloat16
VMEM = pl.BlockSpec(memory_space=pltpu.VMEM)
HBM = pl.BlockSpec(memory_space=pl.ANY)


def far_tiles(blocks):
    low, high = [], []
    for col in range(HALO, REACH + BAND):
        low.append((col, list(range(max(0, col - BAND), REACH))))
    for col in range(blocks - 1 - HALO, blocks - 1 - REACH - BAND, -1):
        high.append((col, list(range(blocks - REACH, min(blocks, col + BAND + 1)))))
    return low, high


def far_count():
    reach = REACH + BAND - HALO
    return reach * (reach + 1) // 2


def centred(panels_ref, b):
    panel = panels_ref[:, b * BS : (b + 1) * BS].astype(F32)
    mean = jnp.sum(panel, axis=0, keepdims=True) * (1.0 / panel.shape[0])
    return (panel - mean).astype(BF16)


def pair_into(pair_ref, slot, panel):
    frames = panel.shape[0]
    pair_ref[slot, :, :BS] = panel
    pair_ref[slot, : frames - LAG, BS:] = panel[LAG:]
    pair_ref[slot, frames - LAG :, BS:] = jnp.zeros((LAG, BS), BF16)


def block_rows(first, last):
    return slice(first * BS, last * BS)


def copies(key, res, out_i, out_l, sems, base):
    at = lax.shift_right_logical(key, 7) - base
    tile = lax.bitwise_and(key, SLOT - 1)
    return (
        pltpu.make_async_copy(res.at[at, 0], out_i.at[tile], sems.at[tile, 0]),
        pltpu.make_async_copy(res.at[at, 1], out_l.at[tile], sems.at[tile, 1]),
    )


def start_run(meta_ref, first, last, *where):
    @pl.loop(first, last)
    def _(r):
        for copy in copies(meta_ref[r], *where):
            copy.start()


def wait_run(meta_ref, first, last, *where):
    @pl.loop(first, last)
    def _(r):
        for copy in copies(meta_ref[r], *where):
            copy.wait()


def keep(res, at, part, frames):
    res[at, 0] = part[:, :BS] * (1.0 / (frames - 1))
    res[at, 1] = part[:, BS:] * (1.0 / (frames - LAG))


def inner_kernel(
    blocks, groups, tiles, meta_hbm, own_ref, out_i, out_l, edge_l, edge_r, low_ref, high_ref,
    meta_ref, turned, pair, res, far, sems, side_sems
):
    frames = own_ref.shape[0]
    where = (res, out_i, out_l, sems, 0)
    meta_copy = pltpu.make_async_copy(meta_hbm, meta_ref, side_sems.at[2])
    meta_copy.start()

    def ends(group):
        return meta_ref[tiles + group]

    side_copies = [
        pltpu.make_async_copy(pair.at[pl.ds(at, BAND), :, pl.ds(0, BS)], ref, side_sems.at[side])
        for side, (at, ref) in enumerate(((0, edge_l), (blocks - BAND, edge_r)))
    ]
    far_places = [[(row, col) for col, rows in side for row in rows] for side in far_tiles(blocks)]
    ready = 0
    first = 0
    for end in groups:
        for b in range(ready, min(blocks, end + BAND)):
            panel = centred(own_ref, b)
            turned[block_rows(b, b + 1), :] = panel.T
            pair_into(pair, b, panel)
        if ready < blocks <= end + BAND:
            for copy in side_copies:
                copy.start()
        ready = min(blocks, end + BAND)
        for col in range(first, end):
            low, high = max(0, col - BAND), min(blocks, col + BAND + 1)
            prod = jnp.dot(turned[block_rows(low, high), :], pair[col], preferred_element_type=F32)
            for row in range(low, high):
                at = col * SPAN + row - col + BAND
                keep(res, at, prod[block_rows(row - low, row - low + 1)], frames)
                for side, tiles_far in enumerate(far_places):
                    if (row, col) in tiles_far:
                        t = tiles_far.index((row, col))
                        for half in range(2):
                            far[side, block_rows(t, t + 1), half * BS : (half + 1) * BS] = res[at, half].astype(BF16)
        if first == 0:
            meta_copy.wait()
        start_run(meta_ref, ends(first), ends(end), *where)
        first = end
    far_copies = [
        pltpu.make_async_copy(far.at[side], ref, side_sems.at[3 + side]) for side, ref in enumerate((low_ref, high_ref))
    ]
    for copy in far_copies:
        copy.start()
    for copy in side_copies + far_copies:
        copy.wait()
    wait_run(meta_ref, 0, ends(blocks), *where)


def edge_kernel(
    blocks, base, tiles, meta_hbm, edge_l, edge_r, halo_ref, in_i, in_l,
    out_i, out_l, meta_ref, own, turned, pair, res, sems, in_sems,
):
    del in_i, in_l
    frames = halo_ref.shape[0]
    where = (res, out_i, out_l, sems, base)
    halo0, own0, row0 = (0, BAND), (HALO, 0), (HALO - REACH, 0)

    def copy_in(src, dst, at):
        copy = pltpu.make_async_copy(src, dst, in_sems.at[at])
        copy.start()
        return copy

    own_copies = []
    for side, edge_ref in enumerate((edge_l, edge_r)):
        own_copies.append(copy_in(edge_ref, own.at[side], side))
    meta_copy = pltpu.make_async_copy(meta_hbm, meta_ref, in_sems.at[2])
    meta_copy.start()

    def ends(group):
        return meta_ref[tiles + group]

    for side in range(2):

        def place(col, panel):
            pair_into(pair.at[side], col, panel)
            row = col - row0[side]
            if 0 <= row < ROWS:
                turned[side, block_rows(row, row + 1), :] = panel.T

        for b in range(HALO):
            place(halo0[side] + b, centred(halo_ref, side * HALO + b))
        own_copies[side].wait()
        for b in range(BAND):
            place(own0[side] + b, own[side, b])
        for col in range(COLS):
            rows = [row for row in range(ROWS) if abs(row + row0[side] - col) <= BAND]
            if own0[side] <= col < own0[side] + BAND:
                rows = [row for row in rows if (row < REACH if side == 0 else row >= BAND)]
            low, high = rows[0], rows[-1] + 1
            prod = jnp.dot(turned[side, block_rows(low, high), :], pair[side, col], preferred_element_type=F32)
            for row in rows:
                at = (side * ROWS + row) * COLS + col
                keep(res, at, prod[block_rows(row - low, row - low + 1)], frames)
        if side == 0:
            meta_copy.wait()
        start_run(meta_ref, ends(blocks + 1 + side), ends(blocks + 2 + side), *where)
    wait_run(meta_ref, ends(blocks + 1), tiles, *where)


def last_kernel(blocks, base, tiles, meta_hbm, far_l, far_r, in_i, in_l, out_i, out_l, meta_ref, res, sems, meta_sem):
    del in_i, in_l
    where = (res, out_i, out_l, sems, base)
    meta_copy = pltpu.make_async_copy(meta_hbm, meta_ref, meta_sem)
    meta_copy.start()
    count = far_count()
    for other, far in enumerate((far_l, far_r)):
        for t in range(count):
            for half in range(2):
                res[other * count + t, half] = far[block_rows(t, t + 1), half * BS : (half + 1) * BS].astype(F32)
    meta_copy.wait()
    first, last = meta_ref[tiles + blocks], meta_ref[tiles + blocks + 1]
    start_run(meta_ref, first, last, *where)
    wait_run(meta_ref, first, last, *where)


def sorted_keys(tile_list, blocks):
    tiles = tile_list.shape[0]
    rel = tile_list - lax.axis_index(AXES) * blocks
    row, col = rel[:, 0], rel[:, 1]
    inner = col * SPAN + row - col + BAND
    far0 = blocks * SPAN
    reach = REACH + BAND - HALO
    below = -HALO - 1 - col
    above = col - (blocks + HALO)

    def before(step):
        return step * reach - step * (step - 1) // 2

    far_low = far0 + before(below) + row + REACH
    far_high = far0 + far_count() + before(above) + row - (blocks + HALO - BAND) - above
    left0 = far0 + 2 * far_count()
    right0 = left0 + ROWS * COLS
    left = left0 + (row + REACH) * COLS + col + HALO
    right = right0 + (row - (blocks - BAND)) * COLS + col - (blocks - BAND)
    place = jnp.where((row >= blocks) | (col >= blocks), right, inner)
    place = jnp.where((row < 0) | (col < 0), left, place)
    place = jnp.where(below >= 0, far_low, jnp.where(above >= 0, far_high, place))
    key = place * SLOT + lax.iota(jnp.int32, tiles)
    rank = jnp.sum((key[None, :] < key[:, None]).astype(jnp.int32), axis=1)
    keys = jnp.sum(jnp.where(rank[None, :] == lax.iota(jnp.int32, tiles)[:, None], key[None, :], 0), axis=1)
    number = lax.iota(jnp.int32, blocks + 4)
    edges = number * SPAN
    for at, value in ((1, left0), (2, right0), (3, right0 + ROWS * COLS)):
        edges = jnp.where(number == blocks + at, value, edges)
    ends = jnp.sum((key[None, :] < edges[:, None] * SLOT).astype(jnp.int32), axis=1)
    return jnp.concatenate([keys, ends, jnp.zeros((-(tiles + blocks + 4) % SLOT,), jnp.int32)]), far0


def per_device(trajectory, tile_list):
    count = lax.axis_size(AXES)
    parts = trajectory.reshape(trajectory.shape[0], count, -1)
    blocks = parts.shape[2] // BS
    tiles = tile_list.shape[0]
    own = lax.all_to_all(trajectory, AXES, split_axis=1, concat_axis=0, tiled=True)
    frames = own.shape[0]
    edge = HALO * BS
    beside = jnp.concatenate(
        [
            jnp.pad(parts[:, :-1, parts.shape[2] - edge :], ((0, 0), (1, 0), (0, 0))),
            jnp.pad(parts[:, 1:, :edge], ((0, 0), (0, 1), (0, 0))),
        ],
        axis=2,
    )
    meta, base = sorted_keys(tile_list, blocks)
    own, beside, meta = lax.optimization_barrier((own, beside, meta))
    words = pltpu.SMEM(meta.shape, jnp.int32)
    halo = lax.all_to_all(beside, AXES, split_axis=1, concat_axis=0, tiled=True).reshape(frames, 2 * edge)

    far = far_count()
    outs = [jax.ShapeDtypeStruct((tiles, BS, BS), F32)] * 2
    inst, lagg, edge_l, edge_r, to_left, to_right = pl.pallas_call(
        functools.partial(inner_kernel, blocks, (blocks,), tiles),
        out_shape=outs + [jax.ShapeDtypeStruct((BAND, frames, BS), BF16)] * 2
        + [jax.ShapeDtypeStruct((far * BS, 2 * BS), BF16)] * 2,
        in_specs=[HBM, VMEM],
        out_specs=[HBM] * 6,
        scratch_shapes=[
            words,
            pltpu.VMEM((blocks * BS, frames), BF16),
            pltpu.VMEM((blocks, frames, 2 * BS), BF16),
            pltpu.VMEM((blocks * SPAN, 2, BS, BS), F32),
            pltpu.VMEM((2, far * BS, 2 * BS), BF16),
            pltpu.SemaphoreType.DMA((tiles, 2)),
            pltpu.SemaphoreType.DMA((5,)),
        ],
        compiler_params=pltpu.CompilerParams(vmem_limit_bytes=52 << 20),
        cost_estimate=pl.CostEstimate(
            flops=blocks * SPAN * 4 * BS * BS * frames, bytes_accessed=20 << 20, transcendentals=0
        ),
        name="inner_tiles",
    )(meta, own)
    far_r = lax.ppermute(to_left, AXES, [(i + 1, i) for i in range(count - 1)])
    far_l = lax.ppermute(to_right, AXES, [(i, i + 1) for i in range(count - 1)])
    inst, lagg = pl.pallas_call(
        functools.partial(edge_kernel, blocks, base + 2 * far, tiles),
        out_shape=outs,
        in_specs=[HBM, HBM, HBM, VMEM, HBM, HBM],
        out_specs=[HBM, HBM],
        scratch_shapes=[
            words,
            pltpu.VMEM((2, BAND, frames, BS), BF16),
            pltpu.VMEM((2, ROWS * BS, frames), BF16),
            pltpu.VMEM((2, COLS, frames, 2 * BS), BF16),
            pltpu.VMEM((2 * ROWS * COLS, 2, BS, BS), F32),
            pltpu.SemaphoreType.DMA((tiles, 2)),
            pltpu.SemaphoreType.DMA((3,)),
        ],
        input_output_aliases={4: 0, 5: 1},
        compiler_params=pltpu.CompilerParams(vmem_limit_bytes=36 << 20),
        cost_estimate=pl.CostEstimate(flops=50 * 4 * BS * BS * frames, bytes_accessed=16 << 20, transcendentals=0),
        name="edge_tiles",
    )(meta, edge_l, edge_r, halo, inst, lagg)
    inst, lagg = pl.pallas_call(
        functools.partial(last_kernel, blocks, base, tiles),
        out_shape=outs,
        in_specs=[HBM, VMEM, VMEM, HBM, HBM],
        out_specs=[HBM, HBM],
        scratch_shapes=[
            words,
            pltpu.VMEM((2 * far, 2, BS, BS), F32),
            pltpu.SemaphoreType.DMA((tiles, 2)),
            pltpu.SemaphoreType.DMA,
        ],
        input_output_aliases={3: 0, 4: 1},
        compiler_params=pltpu.CompilerParams(vmem_limit_bytes=16 << 20),
        name="last_tiles",
    )(meta, far_l, far_r, inst, lagg)
    return (inst, lagg)


def solution(mesh):
    in_specs = (P(AXES, None), P(AXES, None))
    out_specs = (P(AXES, None, None), P(AXES, None, None))
    return jax.shard_map(per_device, mesh=mesh, in_specs=in_specs, out_specs=out_specs, check_vma=False)
```

```python
import functools

import jax
import jax.numpy as jnp
from jax import lax
from jax.experimental import pallas as pl
from jax.experimental.pallas import tpu as pltpu
from jax.sharding import PartitionSpec as P

BS = 128
LAG = 16
BAND = 4
REACH = 2
HALO = 4
SPAN = 2 * BAND + 1
ROWS = REACH + BAND
COLS = HALO + BAND
KEPT = 16
SLOT = 128
AXES = ("frames", "feat")
F32 = jnp.float32
BF16 = jnp.bfloat16
VMEM = pl.BlockSpec(memory_space=pltpu.VMEM)
HBM = pl.BlockSpec(memory_space=pl.ANY)


def far_tiles(blocks):
    low, high = [], []
    for col in range(HALO, REACH + BAND):
        low.append((col, list(range(max(0, col - BAND), REACH))))
    for col in range(blocks - 1 - HALO, blocks - 1 - REACH - BAND, -1):
        high.append((col, list(range(blocks - REACH, min(blocks, col + BAND + 1)))))
    return low, high


def far_count():
    reach = REACH + BAND - HALO
    return reach * (reach + 1) // 2


def centred(panels_ref, b):
    panel = panels_ref[:, b * BS : (b + 1) * BS].astype(F32)
    mean = jnp.sum(panel, axis=0, keepdims=True) * (1.0 / panel.shape[0])
    return (panel - mean).astype(BF16)


def pair_into(pair_ref, slot, panel):
    frames = panel.shape[0]
    pair_ref[slot, :, :BS] = panel
    pair_ref[slot, : frames - LAG, BS:] = panel[LAG:]
    pair_ref[slot, frames - LAG :, BS:] = jnp.zeros((LAG, BS), BF16)


def block_rows(first, last):
    return slice(first * BS, last * BS)


def copies(key, res, out_i, out_l, sems, base):
    at = lax.shift_right_logical(key, 7) - base
    tile = lax.bitwise_and(key, SLOT - 1)
    return (
        pltpu.make_async_copy(res.at[at, 0], out_i.at[tile], sems.at[tile, 0]),
        pltpu.make_async_copy(res.at[at, 1], out_l.at[tile], sems.at[tile, 1]),
    )


def start_run(meta_ref, first, last, *where):
    @pl.loop(first, last)
    def _(r):
        for copy in copies(meta_ref[r], *where):
            copy.start()


def wait_run(meta_ref, first, last, *where):
    @pl.loop(first, last)
    def _(r):
        for copy in copies(meta_ref[r], *where):
            copy.wait()


def keep(res, at, part, frames):
    res[at, 0] = part[:, :BS] * (1.0 / (frames - 1))
    res[at, 1] = part[:, BS:] * (1.0 / (frames - LAG))


def inner_kernel(
    blocks, groups, tiles, meta_hbm, own_ref, out_i, out_l, edge_ref, low_ref, high_ref,
    meta_ref, turned, pair, res, far, sems, side_sems
):
    frames = own_ref.shape[0]
    where = (res, out_i, out_l, sems, 0)
    meta_copy = pltpu.make_async_copy(meta_hbm, meta_ref, side_sems.at[2])
    meta_copy.start()

    def ends(group):
        return meta_ref[tiles + group]

    side_copies = [
        pltpu.make_async_copy(pair.at[pl.ds(at, BAND), :, pl.ds(0, BS)], edge_ref.at[side], side_sems.at[side])
        for side, at in enumerate((0, blocks - BAND))
    ]
    far_places = [[(row, col) for col, rows in side for row in rows] for side in far_tiles(blocks)]
    ready = 0
    first = 0
    for end in groups:
        for b in range(ready, min(blocks, end + BAND)):
            panel = centred(own_ref, b)
            turned[block_rows(b, b + 1), :] = panel.T
            pair_into(pair, b, panel)
        if ready < blocks <= end + BAND:
            for copy in side_copies:
                copy.start()
        ready = min(blocks, end + BAND)
        for col in range(first, end):
            low, high = max(0, col - BAND), min(blocks, col + BAND + 1)
            prod = jnp.dot(turned[block_rows(low, high), :], pair[col], preferred_element_type=F32)
            for row in range(low, high):
                at = col * SPAN + row - col + BAND
                keep(res, at, prod[block_rows(row - low, row - low + 1)], frames)
                for side, tiles_far in enumerate(far_places):
                    if (row, col) in tiles_far:
                        t = tiles_far.index((row, col))
                        for half in range(2):
                            far[side, block_rows(t, t + 1), half * BS : (half + 1) * BS] = res[at, half].astype(BF16)
        if first == 0:
            meta_copy.wait()
        start_run(meta_ref, ends(first), ends(end), *where)
        first = end
    far_copies = [
        pltpu.make_async_copy(far.at[side], ref, side_sems.at[3 + side]) for side, ref in enumerate((low_ref, high_ref))
    ]
    for copy in far_copies:
        copy.start()
    for copy in side_copies + far_copies:
        copy.wait()
    wait_run(meta_ref, 0, ends(blocks), *where)


def edge_kernel(blocks, side, base, tiles, meta_hbm, edge_ref, halo_ref, *refs):
    far_refs = refs[: 2 * side]
    out_i, out_l, meta_ref, own, turned, pair, res, sems, in_sems = refs[2 * side + 2 :]
    frames = halo_ref.shape[0]
    where = (res, out_i, out_l, sems, base)
    count = far_count() * len(far_refs)
    first_row = -REACH if side == 0 else blocks - BAND

    def block_of(slot):
        if slot < HALO:
            return slot - HALO if side == 0 else blocks + slot
        return slot - HALO + (0 if side == 0 else blocks - BAND)

    own_copy = pltpu.make_async_copy(edge_ref.at[side], own, in_sems.at[0])
    meta_copy = pltpu.make_async_copy(meta_hbm, meta_ref, in_sems.at[1])
    own_copy.start()
    meta_copy.start()

    def ends(group):
        return meta_ref[tiles + group]

    def place(slot):
        panel = centred(halo_ref, side * HALO + slot) if slot < HALO else own[slot - HALO]
        pair_into(pair, slot, panel)
        row = block_of(slot) - first_row
        if 0 <= row < ROWS:
            turned[block_rows(row, row + 1), :] = panel.T

    for other, far in enumerate(far_refs):
        for t in range(far_count()):
            for half in range(2):
                part = far[block_rows(t, t + 1), half * BS : (half + 1) * BS]
                res[other * far_count() + t, half] = part.astype(F32)
    for slot in range(HALO):
        place(slot)
    meta_copy.wait()
    if far_refs:
        start_run(meta_ref, ends(blocks + 2), ends(blocks + 3), *where)
    own_copy.wait()
    for slot in range(HALO, COLS):
        place(slot)
    group = blocks + 3 * side
    for slot in range(COLS):
        col = block_of(slot)
        rows = [row for row in range(ROWS) if abs(row + first_row - col) <= BAND]
        if slot >= HALO:
            rows = [row for row in rows if not 0 <= row + first_row < blocks]
        low, high = rows[0], rows[-1] + 1
        prod = jnp.dot(turned[block_rows(low, high), :], pair[slot], preferred_element_type=F32)
        for row in rows:
            keep(res, count + slot * ROWS + row, prod[block_rows(row - low, row - low + 1)], frames)
        if slot in (HALO - 1, COLS - 1):
            start_run(meta_ref, ends(group), ends(group + 1), *where)
            group += 1
    wait_run(meta_ref, ends(blocks + 2 * side), ends(blocks + 2 + 3 * side), *where)


def sorted_keys(tile_list, blocks):
    tiles = tile_list.shape[0]
    rel = tile_list - lax.axis_index(AXES) * blocks
    row, col = rel[:, 0], rel[:, 1]
    inner = col * SPAN + row - col + BAND
    reach = REACH + BAND - HALO
    below = -HALO - 1 - col
    above = col - (blocks + HALO)

    def before(step):
        return step * reach - step * (step - 1) // 2

    left0 = blocks * SPAN
    far0 = left0 + ROWS * COLS
    right0 = far0 + 2 * far_count()
    far_low = far0 + before(below) + row + REACH
    far_high = far0 + far_count() + before(above) + row - (blocks + HALO - BAND) - above
    left = left0 + (col + HALO) * ROWS + row + REACH
    slot = jnp.where(col >= blocks, col - blocks, col - (blocks - BAND) + HALO)
    right = right0 + slot * ROWS + row - (blocks - BAND)
    place = jnp.where((row >= blocks) | (col >= blocks), right, inner)
    place = jnp.where((row < 0) | (col < 0), left, place)
    place = jnp.where(below >= 0, far_low, jnp.where(above >= 0, far_high, place))
    key = place * SLOT + lax.iota(jnp.int32, tiles)
    rank = jnp.sum((key[None, :] < key[:, None]).astype(jnp.int32), axis=1)
    keys = jnp.sum(jnp.where(rank[None, :] == lax.iota(jnp.int32, tiles)[:, None], key[None, :], 0), axis=1)
    number = lax.iota(jnp.int32, blocks + 6)
    edges = number * SPAN
    starts = (left0 + HALO * ROWS, far0, right0, right0 + HALO * ROWS, right0 + COLS * ROWS)
    for at, value in enumerate(starts):
        edges = jnp.where(number == blocks + 1 + at, value, edges)
    ends = jnp.sum((key[None, :] < edges[:, None] * SLOT).astype(jnp.int32), axis=1)
    return jnp.concatenate([keys, ends, jnp.zeros((-(tiles + blocks + 6) % SLOT,), jnp.int32)]), (left0, far0)


def per_device(trajectory, tile_list):
    count = lax.axis_size(AXES)
    parts = trajectory.reshape(trajectory.shape[0], count, -1)
    blocks = parts.shape[2] // BS
    tiles = tile_list.shape[0]
    own = lax.all_to_all(trajectory, AXES, split_axis=1, concat_axis=0, tiled=True)
    frames = own.shape[0]
    edge = HALO * BS
    beside = jnp.concatenate(
        [
            jnp.pad(parts[:, :-1, parts.shape[2] - edge :], ((0, 0), (1, 0), (0, 0))),
            jnp.pad(parts[:, 1:, :edge], ((0, 0), (0, 1), (0, 0))),
        ],
        axis=2,
    )
    meta, bases = sorted_keys(tile_list, blocks)
    own, beside, meta = lax.optimization_barrier((own, beside, meta))
    words = pltpu.SMEM(meta.shape, jnp.int32)
    halo = lax.all_to_all(beside, AXES, split_axis=1, concat_axis=0, tiled=True).reshape(frames, 2 * edge)

    far = far_count()
    outs = [jax.ShapeDtypeStruct((tiles, BS, BS), F32)] * 2
    inst, lagg, edges, to_left, to_right = pl.pallas_call(
        functools.partial(inner_kernel, blocks, (blocks,), tiles),
        out_shape=outs + [jax.ShapeDtypeStruct((KEPT, BAND, frames, BS), BF16)]
        + [jax.ShapeDtypeStruct((far * BS, 2 * BS), BF16)] * 2,
        in_specs=[HBM, VMEM],
        out_specs=[HBM] * 5,
        scratch_shapes=[
            words,
            pltpu.VMEM((blocks * BS, frames), BF16),
            pltpu.VMEM((blocks, frames, 2 * BS), BF16),
            pltpu.VMEM((blocks * SPAN, 2, BS, BS), F32),
            pltpu.VMEM((2, far * BS, 2 * BS), BF16),
            pltpu.SemaphoreType.DMA((tiles, 2)),
            pltpu.SemaphoreType.DMA((5,)),
        ],
        compiler_params=pltpu.CompilerParams(vmem_limit_bytes=52 << 20),
        cost_estimate=pl.CostEstimate(
            flops=blocks * SPAN * 4 * BS * BS * frames, bytes_accessed=20 << 20, transcendentals=0
        ),
        name="inner_tiles",
    )(meta, own)
    far_r = lax.ppermute(to_left, AXES, [(i + 1, i) for i in range(count - 1)])
    far_l = lax.ppermute(to_right, AXES, [(i, i + 1) for i in range(count - 1)])
    for side, received in enumerate(((), (far_l, far_r))):
        far_tiles_in = far * len(received)
        inst, lagg = pl.pallas_call(
            functools.partial(edge_kernel, blocks, side, bases[side], tiles),
            out_shape=outs,
            in_specs=[HBM, HBM, VMEM] + [VMEM] * len(received) + [HBM, HBM],
            out_specs=[HBM, HBM],
            scratch_shapes=[
                words,
                pltpu.VMEM((BAND, frames, BS), BF16),
                pltpu.VMEM((ROWS * BS, frames), BF16),
                pltpu.VMEM((COLS, frames, 2 * BS), BF16),
                pltpu.VMEM((far_tiles_in + COLS * ROWS, 2, BS, BS), F32),
                pltpu.SemaphoreType.DMA((tiles, 2)),
                pltpu.SemaphoreType.DMA((2,)),
            ],
            input_output_aliases={3 + len(received): 0, 4 + len(received): 1},
            compiler_params=pltpu.CompilerParams(vmem_limit_bytes=48 << 20),
            cost_estimate=pl.CostEstimate(flops=25 * 4 * BS * BS * frames, bytes_accessed=8 << 20, transcendentals=0),
            name=("left_tiles", "right_tiles")[side],
        )(meta, edges, halo, *received, inst, lagg)
    return (inst, lagg)


def solution(mesh):
    in_specs = (P(AXES, None), P(AXES, None))
    out_specs = (P(AXES, None, None), P(AXES, None, None))
    return jax.shard_map(per_device, mesh=mesh, in_specs=in_specs, out_specs=out_specs, check_vma=False)
```

```python
import functools

import jax
import jax.numpy as jnp
from jax import lax
from jax.experimental import pallas as pl
from jax.experimental.pallas import tpu as pltpu
from jax.sharding import PartitionSpec as P

BS = 128
LAG = 16
BAND = 4
REACH = 2
HALO = 4
SPAN = 2 * BAND + 1
ROWS = REACH + BAND
COLS = HALO + BAND
KEPT = 16
SLOT = 128
AXES = ("frames", "feat")
F32 = jnp.float32
BF16 = jnp.bfloat16
VMEM = pl.BlockSpec(memory_space=pltpu.VMEM)
HBM = pl.BlockSpec(memory_space=pl.ANY)


def far_tiles(blocks):
    low, high = [], []
    for col in range(HALO, REACH + BAND):
        low.append((col, list(range(max(0, col - BAND), REACH))))
    for col in range(blocks - 1 - HALO, blocks - 1 - REACH - BAND, -1):
        high.append((col, list(range(blocks - REACH, min(blocks, col + BAND + 1)))))
    return low, high


def far_count():
    reach = REACH + BAND - HALO
    return reach * (reach + 1) // 2


def centred(panels_ref, b):
    panel = panels_ref[:, b * BS : (b + 1) * BS].astype(F32)
    mean = jnp.sum(panel, axis=0, keepdims=True) * (1.0 / panel.shape[0])
    return (panel - mean).astype(BF16)


def pair_into(pair_ref, slot, panel):
    frames = panel.shape[0]
    pair_ref[slot, :, :BS] = panel
    pair_ref[slot, : frames - LAG, BS:] = panel[LAG:]
    pair_ref[slot, frames - LAG :, BS:] = jnp.zeros((LAG, BS), BF16)


def block_rows(first, last):
    return slice(first * BS, last * BS)


def copies(key, res, out_i, out_l, sems, base):
    at = lax.shift_right_logical(key, 7) - base
    tile = lax.bitwise_and(key, SLOT - 1)
    return (
        pltpu.make_async_copy(res.at[at, 0], out_i.at[tile], sems.at[tile, 0]),
        pltpu.make_async_copy(res.at[at, 1], out_l.at[tile], sems.at[tile, 1]),
    )


def start_run(meta_ref, first, last, *where):
    @pl.loop(first, last)
    def _(r):
        for copy in copies(meta_ref[r], *where):
            copy.start()


def wait_run(meta_ref, first, last, *where):
    @pl.loop(first, last)
    def _(r):
        for copy in copies(meta_ref[r], *where):
            copy.wait()


def keep(res, at, part, frames):
    res[at, 0] = part[:, :BS] * (1.0 / (frames - 1))
    res[at, 1] = part[:, BS:] * (1.0 / (frames - LAG))


def inner_kernel(
    blocks, groups, tiles, meta_hbm, own_ref, out_i, out_l, edge_ref, low_ref, high_ref,
    meta_ref, turned, pair, res, far, sems, side_sems
):
    frames = own_ref.shape[0]
    where = (res, out_i, out_l, sems, 0)
    meta_copy = pltpu.make_async_copy(meta_hbm, meta_ref, side_sems.at[2])
    meta_copy.start()

    def ends(group):
        return meta_ref[tiles + group]

    side_copies = [
        pltpu.make_async_copy(pair.at[pl.ds(at, BAND), :, pl.ds(0, BS)], edge_ref.at[side], side_sems.at[side])
        for side, at in enumerate((0, blocks - BAND))
    ]
    far_places = [[(row, col) for col, rows in side for row in rows] for side in far_tiles(blocks)]
    ready = 0
    first = 0
    for end in groups:
        for b in range(ready, min(blocks, end + BAND)):
            panel = centred(own_ref, b)
            turned[block_rows(b, b + 1), :] = panel.T
            pair_into(pair, b, panel)
        if ready < blocks <= end + BAND:
            for copy in side_copies:
                copy.start()
        ready = min(blocks, end + BAND)
        for col in range(first, end):
            low, high = max(0, col - BAND), min(blocks, col + BAND + 1)
            prod = jnp.dot(turned[block_rows(low, high), :], pair[col], preferred_element_type=F32)
            for row in range(low, high):
                at = col * SPAN + row - col + BAND
                keep(res, at, prod[block_rows(row - low, row - low + 1)], frames)
                for side, tiles_far in enumerate(far_places):
                    if (row, col) in tiles_far:
                        t = tiles_far.index((row, col))
                        for half in range(2):
                            far[side, block_rows(t, t + 1), half * BS : (half + 1) * BS] = res[at, half].astype(BF16)
        if first == 0:
            meta_copy.wait()
        start_run(meta_ref, ends(first), ends(end), *where)
        first = end
    far_copies = [
        pltpu.make_async_copy(far.at[side], ref, side_sems.at[3 + side]) for side, ref in enumerate((low_ref, high_ref))
    ]
    for copy in far_copies:
        copy.start()
    for copy in side_copies + far_copies:
        copy.wait()
    wait_run(meta_ref, 0, ends(blocks), *where)


def edge_kernel(blocks, side, base, tiles, meta_hbm, edge_ref, halo_ref, *refs):
    far_refs = refs[: 2 * side]
    out_i, out_l, meta_ref, own, turned, pair, res, sems, in_sems = refs[2 * side + 2 :]
    frames = halo_ref.shape[0]
    where = (res, out_i, out_l, sems, base)
    count = far_count() * len(far_refs)
    first_row = -REACH if side == 0 else blocks - BAND

    def block_of(slot):
        if slot < HALO:
            return slot - HALO if side == 0 else blocks + slot
        return slot - HALO + (0 if side == 0 else blocks - BAND)

    own_copy = pltpu.make_async_copy(edge_ref.at[side], own, in_sems.at[0])
    meta_copy = pltpu.make_async_copy(meta_hbm, meta_ref, in_sems.at[1])
    own_copy.start()
    meta_copy.start()

    def ends(group):
        return meta_ref[tiles + group]

    def place(slot):
        panel = centred(halo_ref, side * HALO + slot) if slot < HALO else own[slot - HALO]
        pair_into(pair, slot, panel)
        row = block_of(slot) - first_row
        if 0 <= row < ROWS:
            turned[block_rows(row, row + 1), :] = panel.T

    for other, far in enumerate(far_refs):
        for t in range(far_count()):
            for half in range(2):
                part = far[block_rows(t, t + 1), half * BS : (half + 1) * BS]
                res[other * far_count() + t, half] = part.astype(F32)
    for slot in range(HALO):
        place(slot)
    meta_copy.wait()
    if far_refs:
        start_run(meta_ref, ends(blocks + 2), ends(blocks + 3), *where)
    own_copy.wait()
    for slot in range(HALO, COLS):
        place(slot)
    group = blocks + 3 * side
    for slot in range(COLS):
        col = block_of(slot)
        rows = [row for row in range(ROWS) if abs(row + first_row - col) <= BAND]
        if slot >= HALO:
            rows = [row for row in rows if not 0 <= row + first_row < blocks]
        low, high = rows[0], rows[-1] + 1
        prod = jnp.dot(turned[block_rows(low, high), :], pair[slot], preferred_element_type=F32)
        for row in rows:
            keep(res, count + slot * ROWS + row, prod[block_rows(row - low, row - low + 1)], frames)
        if slot == COLS - 1 or (slot == HALO - 1 and side == 1):
            start_run(meta_ref, ends(group), ends(blocks + 3 * side + (1 if slot < HALO else 2)), *where)
            group += 1
    wait_run(meta_ref, ends(blocks + 2 * side), ends(blocks + 2 + 3 * side), *where)


def sorted_keys(tile_list, blocks):
    tiles = tile_list.shape[0]
    rel = tile_list - lax.axis_index(AXES) * blocks
    row, col = rel[:, 0], rel[:, 1]
    inner = col * SPAN + row - col + BAND
    reach = REACH + BAND - HALO
    below = -HALO - 1 - col
    above = col - (blocks + HALO)

    def before(step):
        return step * reach - step * (step - 1) // 2

    left0 = blocks * SPAN
    far0 = left0 + ROWS * COLS
    right0 = far0 + 2 * far_count()
    far_low = far0 + before(below) + row + REACH
    far_high = far0 + far_count() + before(above) + row - (blocks + HALO - BAND) - above
    left = left0 + (col + HALO) * ROWS + row + REACH
    slot = jnp.where(col >= blocks, col - blocks, col - (blocks - BAND) + HALO)
    right = right0 + slot * ROWS + row - (blocks - BAND)
    place = jnp.where((row >= blocks) | (col >= blocks), right, inner)
    place = jnp.where((row < 0) | (col < 0), left, place)
    place = jnp.where(below >= 0, far_low, jnp.where(above >= 0, far_high, place))
    key = place * SLOT + lax.iota(jnp.int32, tiles)
    rank = jnp.sum((key[None, :] < key[:, None]).astype(jnp.int32), axis=1)
    keys = jnp.sum(jnp.where(rank[None, :] == lax.iota(jnp.int32, tiles)[:, None], key[None, :], 0), axis=1)
    number = lax.iota(jnp.int32, blocks + 6)
    edges = number * SPAN
    starts = (left0 + HALO * ROWS, far0, right0, right0 + HALO * ROWS, right0 + COLS * ROWS)
    for at, value in enumerate(starts):
        edges = jnp.where(number == blocks + 1 + at, value, edges)
    ends = jnp.sum((key[None, :] < edges[:, None] * SLOT).astype(jnp.int32), axis=1)
    return jnp.concatenate([keys, ends, jnp.zeros((-(tiles + blocks + 6) % SLOT,), jnp.int32)]), (left0, far0)


def per_device(trajectory, tile_list):
    count = lax.axis_size(AXES)
    parts = trajectory.reshape(trajectory.shape[0], count, -1)
    blocks = parts.shape[2] // BS
    tiles = tile_list.shape[0]
    own = lax.all_to_all(trajectory, AXES, split_axis=1, concat_axis=0, tiled=True)
    frames = own.shape[0]
    edge = HALO * BS
    beside = jnp.concatenate(
        [
            jnp.pad(parts[:, :-1, parts.shape[2] - edge :], ((0, 0), (1, 0), (0, 0))),
            jnp.pad(parts[:, 1:, :edge], ((0, 0), (0, 1), (0, 0))),
        ],
        axis=2,
    )
    meta, bases = sorted_keys(tile_list, blocks)
    own, beside, meta = lax.optimization_barrier((own, beside, meta))
    words = pltpu.SMEM(meta.shape, jnp.int32)
    halo = lax.all_to_all(beside, AXES, split_axis=1, concat_axis=0, tiled=True).reshape(frames, 2 * edge)

    far = far_count()
    outs = [jax.ShapeDtypeStruct((tiles, BS, BS), F32)] * 2
    inst, lagg, edges, to_left, to_right = pl.pallas_call(
        functools.partial(inner_kernel, blocks, (blocks,), tiles),
        out_shape=outs + [jax.ShapeDtypeStruct((KEPT, BAND, frames, BS), BF16)]
        + [jax.ShapeDtypeStruct((far * BS, 2 * BS), BF16)] * 2,
        in_specs=[HBM, VMEM],
        out_specs=[HBM] * 5,
        scratch_shapes=[
            words,
            pltpu.VMEM((blocks * BS, frames), BF16),
            pltpu.VMEM((blocks, frames, 2 * BS), BF16),
            pltpu.VMEM((blocks * SPAN, 2, BS, BS), F32),
            pltpu.VMEM((2, far * BS, 2 * BS), BF16),
            pltpu.SemaphoreType.DMA((tiles, 2)),
            pltpu.SemaphoreType.DMA((5,)),
        ],
        compiler_params=pltpu.CompilerParams(vmem_limit_bytes=52 << 20),
        cost_estimate=pl.CostEstimate(
            flops=blocks * SPAN * 4 * BS * BS * frames, bytes_accessed=20 << 20, transcendentals=0
        ),
        name="inner_tiles",
    )(meta, own)
    far_r = lax.ppermute(to_left, AXES, [(i + 1, i) for i in range(count - 1)])
    far_l = lax.ppermute(to_right, AXES, [(i, i + 1) for i in range(count - 1)])
    for side, received in enumerate(((), (far_l, far_r))):
        far_tiles_in = far * len(received)
        inst, lagg = pl.pallas_call(
            functools.partial(edge_kernel, blocks, side, bases[side], tiles),
            out_shape=outs,
            in_specs=[HBM, HBM, VMEM] + [VMEM] * len(received) + [HBM, HBM],
            out_specs=[HBM, HBM],
            scratch_shapes=[
                words,
                pltpu.VMEM((BAND, frames, BS), BF16),
                pltpu.VMEM((ROWS * BS, frames), BF16),
                pltpu.VMEM((COLS, frames, 2 * BS), BF16),
                pltpu.VMEM((far_tiles_in + COLS * ROWS, 2, BS, BS), F32),
                pltpu.SemaphoreType.DMA((tiles, 2)),
                pltpu.SemaphoreType.DMA((2,)),
            ],
            input_output_aliases={3 + len(received): 0, 4 + len(received): 1},
            compiler_params=pltpu.CompilerParams(vmem_limit_bytes=48 << 20),
            cost_estimate=pl.CostEstimate(flops=25 * 4 * BS * BS * frames, bytes_accessed=8 << 20, transcendentals=0),
            name=("left_tiles", "right_tiles")[side],
        )(meta, edges, halo, *received, inst, lagg)
    return (inst, lagg)


def solution(mesh):
    in_specs = (P(AXES, None), P(AXES, None))
    out_specs = (P(AXES, None, None), P(AXES, None, None))
    return jax.shard_map(per_device, mesh=mesh, in_specs=in_specs, out_specs=out_specs, check_vma=False)
```
